512 devices in a mesh: seq: 128 (over y, z, core), head: 4 (over x).
Axes of the slice: x: 4, y: 8, z: 8, core: 2. Of those that a mesh axis runs over, the one named last changes fastest.
Arguments:
- queries: bfloat16 [131072, 512], P('seq', 'head'), may hold values from -6 to 6
- keys: bfloat16 [131072, 512], P('seq', 'head'), may hold values from -6 to 6
- values: bfloat16 [131072, 512], P('seq', 'head'), may hold values from -6 to 6
- out_grad: bfloat16 [131072, 512], P('seq', 'head'), may hold values from -6 to 6
- lengths: int32 [64], replicated, may hold values from 1 to 3072, 131072 in all
- w_proj: bfloat16 [3, 512, 512], P(None, None, 'head'), may hold values from -0.25 to 0.25
Outputs:
- d_input: float32 [131072, 512], P(('seq', 'head'))
The draws below stay inside these ranges and needn't reach their ends.
Inputs may be any that keep to these rules, and one draw needn't show every extreme that they name: The lengths sum to 131072; the longest is exactly 3072.
All inputs are finite; a program needn't handle non-finite values.
Results may differ from the reference program's by a relative error of at most 0.006.
Values may be sent and summed in bfloat16 or wider, within the bound.
A program may use at most 64 MiB of HBM per device.

```python
import math
import jax
import jax.numpy as jnp
import numpy as np
from jax import lax

D = 512
HEAD = 128
ROWS = 1024
LAGS = 4
TOKENS = 131072
USERS = 64
MAXLEN = 3072


def shard_levels(key, dims, cuts, smallest, largest):
    level, own = 1.0, jax.random.fold_in(key, 6)
    for dim, blocks in cuts:
        draws = jnp.exp(jax.random.uniform(jax.random.fold_in(own, dim), (blocks,), jnp.float32, smallest / len(cuts), largest / len(cuts)))
        level = level * jnp.repeat(draws, dims[dim] // blocks).reshape([-1 if axis == dim else 1 for axis in range(len(dims))])
    return level


def profile(number_of, total, reach, slope):
    portions = [(1 << 20) // math.isqrt(standing ** slope) + 1 for standing in range(2, number_of + 1)]
    spare, holding = total - reach - (number_of - 1), [1] * (number_of - 1)
    while spare > 0:
        movable = [i for i in range(number_of - 1) if holding[i] < reach]
        pool, budget = sum([portions[i] for i in movable]), spare
        for i in movable:
            extra = min(reach - holding[i], max(1, budget * portions[i] // pool), spare)
            holding[i] = holding[i] + extra
            spare = spare - extra
    return np.array([reach] + holding)


def ragged(key, amount, total, limit, skew):
    if amount == 2:
        one = jax.random.randint(key, (), max(1, total - limit), min(limit, total - 1) + 1)
        return jnp.stack([one, total - one])
    sizes = jnp.asarray(profile(amount, total, limit, skew), jnp.int32)
    couples = (amount - 1) // 2
    donor, receiver = sizes[1:1 + 2 * couples:2], sizes[2:2 + 2 * couples:2]
    margin = jnp.minimum(donor - 1, limit - receiver)
    moved = jax.random.randint(jax.random.fold_in(key, 1), (couples,), 0, 1 << 20) % (margin + 1)
    sizes = sizes.at[1:1 + 2 * couples:2].set(donor - moved).at[2:2 + 2 * couples:2].set(receiver + moved)
    return sizes[jax.random.permutation(jax.random.fold_in(key, 2), amount)]


def bell_draw(rng, extent, scale, bound, pieces=(), held_as=jnp.bfloat16):
    entries = jax.random.normal(rng, extent, jnp.float32) * scale
    if len(pieces) > 0:
        entries = shard_levels(rng, extent, pieces, -0.22, 0.18) * entries
    return jnp.clip(entries, min=-bound, max=bound).astype(held_as)


def setup_inputs(seed: int = 0) -> dict:
    key_list = jax.random.split(jax.random.key(seed), 7)
    return {
        "queries": bell_draw(key_list[0], (TOKENS, D), 1.0, 6.0, ((0, 128), (1, 4))),
        "keys": bell_draw(key_list[1], (TOKENS, D), 1.0, 6.0, ((0, 128), (1, 4))),
        "values": bell_draw(key_list[2], (TOKENS, D), 1.0, 6.0, ((0, 128), (1, 4))),
        "out_grad": bell_draw(key_list[3], (TOKENS, D), 1.0, 6.0, ((0, 128), (1, 4))),
        "lengths": ragged(key_list[4], USERS, TOKENS, MAXLEN, 2).astype(jnp.int32),
        "w_proj": bell_draw(key_list[5], (3, D, D), D ** -0.5, 0.25, ((2, 4),)),
    }


def pair_task(query_tile, grad_tile, key_tile, value_tile, query_start, key_start, user_ends):
    tile_rows = query_tile.shape[0]
    score_scale = HEAD ** (-0.5)
    norm_factor = 1.0 / math.sqrt(MAXLEN)
    offsets = lax.iota(jnp.int32, tile_rows)
    query_pos = query_start + offsets
    key_pos = key_start + offsets
    query_user = lax.optimization_barrier(jnp.sum((user_ends[None, :] <= query_pos[:, None]).astype(jnp.int32), axis=1))
    key_user = lax.optimization_barrier(jnp.sum((user_ends[None, :] <= key_pos[:, None]).astype(jnp.int32), axis=1))
    visible = (key_pos[None, :] <= query_pos[:, None]) & (query_user[:, None] == key_user[None, :])
    visible = visible[None, :, :]
    query_wide = query_tile.astype(jnp.float32)
    grad_wide = grad_tile.astype(jnp.float32)
    key_wide = key_tile.astype(jnp.float32)
    value_wide = value_tile.astype(jnp.float32)
    highest = lax.Precision.HIGHEST
    scores = jnp.einsum('qnh,knh->nqk', query_wide, key_wide, precision=highest) * score_scale
    gate_prob = jax.nn.sigmoid(scores)
    weights = jnp.where(visible, scores * gate_prob * norm_factor, 0.0).astype(jnp.bfloat16)
    d_weights = jnp.einsum('qnh,knh->nqk', grad_wide, value_wide, precision=highest)
    d_scores = jnp.where(visible, d_weights * gate_prob * (1.0 + scores * (1.0 - gate_prob)) * norm_factor, 0.0).astype(jnp.bfloat16)
    d_scores_wide = d_scores.astype(jnp.float32)
    weights_wide = weights.astype(jnp.float32)
    query_grad = (jnp.einsum('nqk,knh->qnh', d_scores_wide, key_wide, precision=highest) * score_scale).astype(jnp.bfloat16)
    key_grad = (jnp.einsum('nqk,qnh->knh', d_scores_wide, query_wide, precision=highest) * score_scale).astype(jnp.bfloat16)
    value_grad = jnp.einsum('nqk,qnh->knh', weights_wide, grad_wide, precision=highest).astype(jnp.bfloat16)
    return (query_grad, jnp.stack([key_grad, value_grad]))

def reference(queries, keys, values, out_grad, lengths, w_proj):
    heads = D // HEAD
    tile_count = TOKENS // ROWS
    user_ends = jnp.cumsum(lengths).astype(jnp.int32)
    tiled = (tile_count, ROWS, heads, HEAD)
    query_tiles = queries.reshape(tiled)
    key_tiles = keys.reshape(tiled)
    value_tiles = values.reshape(tiled)
    grad_tiles = out_grad.reshape(tiled)

    def last_user(position):
        return jnp.sum((user_ends <= position).astype(jnp.int32))

    def per_tile(pair_acc, tile_index):
        query_start = tile_index * ROWS
        query_tile = lax.dynamic_index_in_dim(query_tiles, tile_index, 0, keepdims=False)
        grad_tile = lax.dynamic_index_in_dim(grad_tiles, tile_index, 0, keepdims=False)
        query_total = jnp.zeros((ROWS, heads, HEAD), jnp.float32)
        zero_parts = (jnp.zeros((ROWS, heads, HEAD), jnp.bfloat16), jnp.zeros((2, ROWS, heads, HEAD), jnp.bfloat16))
        for offset in range(LAGS):
            key_index = tile_index - offset
            safe_index = jnp.maximum(key_index, 0)
            key_start = key_index * ROWS
            if offset == 0:
                live = key_index >= 0
            else:
                live = (key_index >= 0) & (last_user(query_start) == last_user(key_start + ROWS - 1))
            key_tile = lax.dynamic_index_in_dim(key_tiles, safe_index, 0, keepdims=False)
            value_tile = lax.dynamic_index_in_dim(value_tiles, safe_index, 0, keepdims=False)
            parts = lax.cond(live, lambda: pair_task(query_tile, grad_tile, key_tile, value_tile, query_start, key_start, user_ends), lambda: zero_parts)
            query_total = query_total + parts[0].astype(jnp.float32)
            pair_acc = pair_acc.at[safe_index].add(parts[1].astype(jnp.float32))
        return (pair_acc, query_total)
    start_acc = jnp.zeros((tile_count, 2, ROWS, heads, HEAD), jnp.float32)
    pair_acc, query_totals = lax.scan(per_tile, start_acc, jnp.arange(tile_count, dtype=jnp.int32))
    query_full = query_totals.reshape(TOKENS, D).astype(jnp.bfloat16)
    pair_full = jnp.transpose(pair_acc, (1, 0, 2, 3, 4)).reshape(2, TOKENS, D).astype(jnp.bfloat16)
    d_input = jnp.dot(query_full, w_proj[0].T, preferred_element_type=jnp.float32)
    d_input = d_input + jnp.dot(pair_full[0], w_proj[1].T, preferred_element_type=jnp.float32)
    d_input = d_input + jnp.dot(pair_full[1], w_proj[2].T, preferred_element_type=jnp.float32)
    return d_input
```

```python
import functools
import math

import jax
import jax.numpy as jnp
from jax import lax
from jax.experimental import pallas as pl
from jax.experimental.pallas import tpu as pltpu
from jax.sharding import PartitionSpec as P

MAXLEN = 3072
CHUNKS = 4
FAR = 8192.0
F32 = jnp.float32
BF16 = jnp.bfloat16
NT = (((1,), (1,)), ((), ()))
NN = (((1,), (0,)), ((), ()))
TN = (((0,), (0,)), ((), ()))


def dot(a, b, dims):
    return lax.dot_general(a, b, dims, preferred_element_type=F32)


def beside(a, b):
    return jnp.concatenate([a, b], axis=1)


def kernel(
    seq_n, head_n,
    q_in, k_in, v_in, g_in, len_in, w_in,
    out_ref,
    kv, qg, ka, qa, dq, dk, dv, gs, gr, wg,
    load_sem, kv_send, qg_send, kv_recv, qg_recv, w_send, w_recv, g_send, g_recv,
):
    rows, width = q_in.shape
    chunk = rows // CHUNKS
    scale = width ** -0.5
    norm = 1.0 / math.sqrt(MAXLEN)
    me = lax.axis_index("seq")
    head = lax.axis_index("head")
    even = lax.rem(me, 2) == 0
    odd = lax.rem(me, 2) == 1

    def at(step):
        return lax.rem(me + step + seq_n, seq_n)

    def other(step):
        return lax.rem(head + step, head_n)

    loads = [
        pltpu.make_async_copy(k_in, kv.at[0, 0], load_sem.at[0]),
        pltpu.make_async_copy(v_in, kv.at[0, 1], load_sem.at[1]),
        pltpu.make_async_copy(q_in, qg.at[0, 0], load_sem.at[2]),
        pltpu.make_async_copy(g_in, qg.at[0, 1], load_sem.at[3]),
    ] + [
        pltpu.make_async_copy(
            w_in.at[c], wg.at[head, :, pl.ds(c * width, width)], load_sem.at[4 + c]
        )
        for c in range(3)
    ]
    for load in loads:
        load.start()

    barrier = pltpu.get_barrier_semaphore()
    for step in (-2, -1, 1, 2):
        pl.semaphore_signal(
            barrier, inc=1, device_id=(at(step), head), device_id_type=pl.DeviceIdType.MESH
        )
    for step in range(1, head_n):
        pl.semaphore_signal(
            barrier, inc=1, device_id=(me, other(step)), device_id_type=pl.DeviceIdType.MESH
        )
    pl.semaphore_wait(barrier, 4 + head_n - 1)

    def send(src, dst, send_sem, recv_sem, seq_to, head_to):
        return pltpu.make_async_remote_copy(
            src_ref=src, dst_ref=dst, send_sem=send_sem, recv_sem=recv_sem,
            device_id=(seq_to, head_to), device_id_type=pl.DeviceIdType.MESH,
        )

    def part(buf, lag, j):
        return buf.at[lag, :, pl.ds(j * chunk, chunk), :]

    def kv_copy(kind, j):
        src, dst, step = ((0, 2, 2), (0, 1, 1), (2, 3, 1), (2, 1, -1))[kind]
        return send(part(kv, src, j), part(kv, dst, j), kv_send.at[kind, j], kv_recv.at[dst, j], at(step), head)

    def qg_copy(kind, j):
        src, dst, step = ((0, 2, -2), (0, 1, -1), (2, 3, -1), (2, 1, 1))[kind]
        return send(part(qg, src, j), part(qg, dst, j), qg_send.at[kind, j], qg_recv.at[dst, j], at(step), head)

    def kv_arrived(lag, j):
        kv_copy({1: 1, 2: 0, 3: 2}[lag], j).wait_recv()

    def qg_arrived(lag, j):
        qg_copy({1: 1, 2: 0, 3: 2}[lag], j).wait_recv()

    for load in loads[:4]:
        load.wait()
    for n in range(CHUNKS):
        kv_copy(0, CHUNKS - 1 - n).start()
        qg_copy(0, n).start()

    @pl.when(even)
    def _():
        for n in range(CHUNKS):
            kv_copy(1, CHUNKS - 1 - n).start()

    @pl.when(odd)
    def _():
        for n in range(CHUNKS):
            qg_copy(1, n).start()

    for load in loads[4:]:
        load.wait()

    def w_copy(step, place):
        return send(wg.at[place], wg.at[place], w_send.at[step - 1], w_recv.at[place], me, other(step))

    for step in range(1, head_n):
        w_copy(step, head).start()

    lane = lax.broadcasted_iota(jnp.int32, (1, width), 1)

    def user_step(u, carry):
        end, starts, ends = carry
        later = end + len_in[u]
        return (later, jnp.where(lane == u, end, starts), jnp.where(lane == u, later, ends))

    zero = jnp.zeros((1, width), jnp.int32)
    _, starts, ends = lax.fori_loop(0, len_in.shape[0], user_step, (jnp.int32(0), zero, zero))
    offsets = lax.broadcasted_iota(jnp.int32, (rows, width), 0)

    def belongs(step):
        pos = offsets + at(step) * rows
        return (pos >= starts) & (pos < ends)

    for lag in range(4):
        ka[lag] = jnp.where(belongs(-lag), 0.0, -FAR).astype(BF16)
        qa[lag] = jnp.where(belongs(lag), 1.0, 0.0).astype(BF16)

    def gates(scores, d_weights):
        s = scores * scale
        p = jax.nn.sigmoid(s)
        a = s * p
        ds = (p + a * (1.0 - p)) * d_weights
        return a.astype(BF16), ds.astype(BF16)

    def query_side(lag, j, r0, r1):
        here = pl.ds(j * chunk, chunk)
        own = slice(r0, r1)
        keys = kv[lag, 0, here, :]
        s = dot(beside(qg[0, 0, own, :], qa[0, own, :]), beside(keys, ka[lag, here, :]), NT)
        d = dot(qg[0, 1, own, :], kv[lag, 1, here, :], NT)
        _, ds = gates(s, d)
        dq[own, :] += dot(ds, keys, NN)

    def key_side(lag, j, r0, r1):
        here = pl.ds(j * chunk, chunk)
        own = slice(r0, r1)
        queries = qg[lag, 0, here, :]
        grads = qg[lag, 1, here, :]
        s = dot(beside(kv[0, 0, own, :], ka[0, own, :]), beside(queries, qa[lag, here, :]), NT)
        d = dot(kv[0, 1, own, :], grads, NT)
        a, ds = gates(s, d)
        dk[own, :] += dot(ds, queries, NN)
        dv[own, :] += dot(a, grads, NN)

    tri = lax.broadcasted_iota(jnp.int32, (chunk, chunk), 0) <= lax.broadcasted_iota(
        jnp.int32, (chunk, chunk), 1
    )
    dk[...] = jnp.zeros_like(dk)
    dv[...] = jnp.zeros_like(dv)
    for j in range(CHUNKS):
        here = slice(j * chunk, (j + 1) * chunk)
        upto = slice(0, (j + 1) * chunk)
        queries = qg[0, 0, here, :]
        grads = qg[0, 1, here, :]
        keys = kv[0, 0, upto, :]
        s = dot(beside(keys, ka[0, upto, :]), beside(queries, qa[0, here, :]), NT)
        last = jnp.where(tri, s[j * chunk :, :], -FAR)
        s = last if j == 0 else jnp.concatenate([s[: j * chunk, :], last], axis=0)
        d = dot(kv[0, 1, upto, :], grads, NT)
        a, ds = gates(s, d)
        dk[upto, :] += dot(ds, queries, NN)
        dv[upto, :] += dot(a, grads, NN)
        dq[here, :] = dot(ds, keys, TN)

    def first(n, _):
        jk, jq = CHUNKS - 1 - n, n
        kv_arrived(2, jk)
        kv_copy(2, jk).start()
        pl.when(odd)(lambda: kv_copy(3, jk).start())
        qg_arrived(2, jq)
        qg_copy(2, jq).start()
        pl.when(even)(lambda: qg_copy(3, jq).start())

        @pl.when(odd)
        def _():
            kv_arrived(1, jk)
            query_side(1, jk, 0, rows)

        @pl.when(even)
        def _():
            qg_arrived(1, jq)
            key_side(1, jq, 0, rows)

        query_side(2, jk, 0, rows)
        key_side(2, jq, 0, rows)
        return 0

    lax.fori_loop(0, CHUNKS, first, 0)

    def second(n, _):
        jk, jq = CHUNKS - 1 - n, n

        @pl.when(even)
        def _():
            kv_arrived(1, jk)
            query_side(1, jk, 0, rows)

        @pl.when(odd)
        def _():
            qg_arrived(1, jq)
            key_side(1, jq, 0, rows)

        return 0

    lax.fori_loop(0, CHUNKS, second, 0)

    wide = {0: (0, 1), 1: (1, 2)}

    def g_copy(which, r, place, to):
        first_col, cols = wide[which]
        span = pl.ds(first_col * width, cols * width)
        return send(
            gs.at[r, :, span], gr.at[place, :, span],
            g_send.at[which, r], g_recv.at[which, place], me, to,
        )

    def hand_over(which, r, value):
        first_col, cols = wide[which]
        span = slice(first_col * width, (first_col + cols) * width)

        @pl.when(head == r)
        def _():
            gr[head, :, span] = value

        @pl.when(head != r)
        def _():
            gs[r, :, span] = value
            g_copy(which, r, head, r).start()

    for n in range(CHUNKS):
        jk, jq = CHUNKS - 1 - n, n
        kv_arrived(3, jk)
        query_side(3, jk, 0, (jk + 1) * chunk)
        own = slice(jk * chunk, (jk + 1) * chunk)
        hand_over(0, jk, (dq[own, :] * (scale * norm)).astype(BF16))
        qg_arrived(3, jq)
        key_side(3, jq, jq * chunk, rows)
        own = slice(jq * chunk, (jq + 1) * chunk)
        hand_over(
            1, jq,
            beside((dk[own, :] * (scale * norm)).astype(BF16), (dv[own, :] * norm).astype(BF16)),
        )

    for step in range(1, head_n):
        w_copy(step, other(head_n - step)).wait_recv()
    total = dot(gr[head], wg[head], NT)
    for step in range(1, head_n):
        place = other(step)
        for which in (0, 1):
            g_copy(which, 0, place, place).wait_recv()
        total += dot(gr[place], wg[place], NT)
    out_ref[...] = total

    for step in range(1, head_n):
        w_copy(step, head).wait_send()
        for which in (0, 1):
            g_copy(which, other(step), head, other(step)).wait_send()
    for j in range(CHUNKS):
        for copy in (kv_copy, qg_copy):
            copy(0, j).wait_send()
            copy(2, j).wait_send()

    @pl.when(even)
    def _():
        for j in range(CHUNKS):
            kv_copy(1, j).wait_send()
            qg_copy(3, j).wait_send()

    @pl.when(odd)
    def _():
        for j in range(CHUNKS):
            kv_copy(3, j).wait_send()
            qg_copy(1, j).wait_send()


def shards(seq_n, head_n, queries, keys, values, out_grad, lengths, w_proj):
    rows, width = queries.shape
    model = w_proj.shape[1]
    hbm = pl.BlockSpec(memory_space=pl.ANY)
    dma = pltpu.SemaphoreType.DMA
    return pl.pallas_call(
        functools.partial(kernel, seq_n, head_n),
        out_shape=jax.ShapeDtypeStruct((rows // head_n, model), F32),
        in_specs=[hbm] * 4 + [pl.BlockSpec(memory_space=pltpu.SMEM), hbm],
        out_specs=pl.BlockSpec(memory_space=pltpu.VMEM),
        scratch_shapes=[
            pltpu.VMEM((4, 2, rows, width), BF16),
            pltpu.VMEM((4, 2, rows, width), BF16),
            pltpu.VMEM((4, rows, width), BF16),
            pltpu.VMEM((4, rows, width), BF16),
            pltpu.VMEM((rows, width), F32),
            pltpu.VMEM((rows, width), F32),
            pltpu.VMEM((rows, width), F32),
            pltpu.VMEM((head_n, rows // head_n, 3 * width), BF16),
            pltpu.VMEM((head_n, rows // head_n, 3 * width), BF16),
            pltpu.VMEM((head_n, model, 3 * width), BF16),
            dma((7,)),
            dma((4, CHUNKS)),
            dma((4, CHUNKS)),
            dma((4, CHUNKS)),
            dma((4, CHUNKS)),
            dma((head_n - 1,)),
            dma((head_n,)),
            dma((2, head_n)),
            dma((2, head_n)),
        ],
        compiler_params=pltpu.CompilerParams(
            collective_id=0, has_side_effects=True, vmem_limit_bytes=48 << 20
        ),
    )(queries, keys, values, out_grad, lengths, w_proj)


def solution(mesh):
    return jax.shard_map(
        functools.partial(shards, mesh.shape["seq"], mesh.shape["head"]),
        mesh=mesh,
        in_specs=(
            P("seq", "head"),
            P("seq", "head"),
            P("seq", "head"),
            P("seq", "head"),
            P(),
            P(None, None, "head"),
        ),
        out_specs=P(("seq", "head"), None),
        check_vma=False,
    )
```

```python
import functools
import math

import jax
import jax.numpy as jnp
from jax import lax
from jax.experimental import pallas as pl
from jax.experimental.pallas import tpu as pltpu
from jax.sharding import PartitionSpec as P

MAXLEN = 3072
CHUNKS = 4
FAR = 8192.0
F32 = jnp.float32
BF16 = jnp.bfloat16
NT = (((1,), (1,)), ((), ()))
NN = (((1,), (0,)), ((), ()))
TN = (((0,), (0,)), ((), ()))


def dot(a, b, dims):
    return lax.dot_general(a, b, dims, preferred_element_type=F32)


def beside(a, b):
    return jnp.concatenate([a, b], axis=1)


def kernel(
    seq_n, head_n,
    q_in, k_in, v_in, g_in, len_in, w_in,
    out_ref,
    kv, qg, ka, qa, dq, dk, dv, dq_out, dq_in, gs, gr, wg,
    load_sem, qg_send, qg_recv, dq_send, dq_recv, w_send, w_recv, g_send, g_recv,
):
    rows, width = q_in.shape
    chunk = rows // CHUNKS
    scale = width ** -0.5
    norm = 1.0 / math.sqrt(MAXLEN)
    me = lax.axis_index("seq")
    head = lax.axis_index("head")
    even = lax.rem(me, 2) == 0
    odd = lax.rem(me, 2) == 1

    def exists(step):
        return (me + step >= 0) & (me + step < seq_n)

    def other(step):
        return lax.rem(head + step, head_n)

    loads = [
        pltpu.make_async_copy(k_in, kv.at[0], load_sem.at[0]),
        pltpu.make_async_copy(v_in, kv.at[1], load_sem.at[1]),
        pltpu.make_async_copy(q_in, qg.at[0, 0], load_sem.at[2]),
        pltpu.make_async_copy(g_in, qg.at[0, 1], load_sem.at[3]),
    ] + [
        pltpu.make_async_copy(
            w_in.at[c], wg.at[head, :, pl.ds(c * width, width)], load_sem.at[4 + c]
        )
        for c in range(3)
    ]
    for load in loads:
        load.start()

    barrier = pltpu.get_barrier_semaphore()
    for step in (-3, -2, -1, 1, 2, 3):

        @pl.when(exists(step))
        def _():
            pl.semaphore_signal(
                barrier, inc=1, device_id=(me + step, head), device_id_type=pl.DeviceIdType.MESH
            )

    for step in range(1, head_n):
        pl.semaphore_signal(
            barrier, inc=1, device_id=(me, other(step)), device_id_type=pl.DeviceIdType.MESH
        )
    missing = jnp.maximum(3 - me, 0) + jnp.maximum(me + 4 - seq_n, 0)
    pl.semaphore_wait(barrier, 6 + head_n - 1 - missing)

    def send(src, dst, send_sem, recv_sem, seq_to, head_to):
        return pltpu.make_async_remote_copy(
            src_ref=src, dst_ref=dst, send_sem=send_sem, recv_sem=recv_sem,
            device_id=(seq_to, head_to), device_id_type=pl.DeviceIdType.MESH,
        )

    def part(buf, lag, j):
        return buf.at[lag, :, pl.ds(j * chunk, chunk), :]

    def qg_copy(kind, j):
        src, dst, step = ((0, 2, -2), (0, 1, -1), (2, 3, -1), (2, 1, 1))[kind]
        return send(part(qg, src, j), part(qg, dst, j), qg_send.at[kind, j], qg_recv.at[dst, j], me + step, head)

    def qg_arrived(lag, j):
        pl.when(exists(lag))(lambda: qg_copy({1: 1, 2: 0, 3: 2}[lag], j).wait_recv())

    def dq_copy(lag, j):
        here = pl.ds(j * chunk, chunk)
        return send(
            dq_out.at[lag - 1, here, :], dq_in.at[lag - 1, here, :],
            dq_send.at[lag - 1, j], dq_recv.at[lag - 1, j], me + lag, head,
        )

    qg_goes = (exists(-2), odd, exists(2) & exists(-1), even & exists(2))
    for load in loads[2:4]:
        load.wait()
    for n in range(CHUNKS):
        pl.when(qg_goes[0])(lambda: qg_copy(0, n).start())
        pl.when(qg_goes[1])(lambda: qg_copy(1, n).start())
    for load in loads[:2] + loads[4:]:
        load.wait()

    core = lax.rem(me, 2)
    half = w_in.shape[1] // 2
    sibling = me + 1 - 2 * core

    def w_part(place, which):
        return wg.at[place, pl.ds(which * half, half), :]

    def w_copy(step, place):
        ref = w_part(place, core)
        return send(ref, ref, w_send.at[0, step - 1], w_recv.at[0, place], me, other(step))

    def w_share(step, place, which):
        ref = w_part(place, which)
        return send(ref, ref, w_send.at[1, step - 1], w_recv.at[1, place], sibling, head)

    for step in range(1, head_n):
        w_copy(step, head).start()

    lane = lax.broadcasted_iota(jnp.int32, (1, width), 1)

    def user_step(u, carry):
        end, starts, ends = carry
        later = end + len_in[u]
        return (later, jnp.where(lane == u, end, starts), jnp.where(lane == u, later, ends))

    zero = jnp.zeros((1, width), jnp.int32)
    _, starts, ends = lax.fori_loop(0, len_in.shape[0], user_step, (jnp.int32(0), zero, zero))
    offsets = lax.broadcasted_iota(jnp.int32, (rows, width), 0)

    def belongs(step):
        pos = offsets + (me + step) * rows
        return (pos >= starts) & (pos < ends)

    ka[...] = jnp.where(belongs(0), 0.0, -FAR).astype(BF16)
    for lag in range(4):
        qa[lag] = jnp.where(belongs(lag), 1.0, 0.0).astype(BF16)

    for lag in range(1, 4):

        @pl.when(jnp.logical_not(exists(-lag)))
        def _():
            dq_in[lag - 1] = jnp.zeros(dq_in.shape[1:], BF16)

        @pl.when(jnp.logical_not(exists(lag)))
        def _():
            qg[lag] = jnp.zeros(qg.shape[1:], BF16)

    def gates(scores, d_weights):
        s = scores * scale
        p = jax.nn.sigmoid(s)
        a = s * p
        ds = (p + a * (1.0 - p)) * d_weights
        return a.astype(BF16), ds.astype(BF16)

    def terms(lag, j, r0, r1):
        here = pl.ds(j * chunk, chunk)
        own = slice(r0, r1)
        queries = qg[lag, 0, here, :]
        grads = qg[lag, 1, here, :]
        keys = kv[0, own, :]
        s = dot(beside(keys, ka[own, :]), beside(queries, qa[lag, here, :]), NT)
        if lag == 0:
            last = jnp.where(tri, s[r1 - chunk :, :], -FAR)
            s = last if r1 == chunk else jnp.concatenate([s[: r1 - chunk, :], last], axis=0)
        d = dot(kv[1, own, :], grads, NT)
        a, ds = gates(s, d)
        dk[own, :] += dot(ds, queries, NN)
        dv[own, :] += dot(a, grads, NN)
        partial = dot(ds, keys, TN) * (scale * norm)
        if lag == 0:
            dq[here, :] = partial
        else:
            dq_out[lag - 1, here, :] = partial.astype(BF16)
            pl.when(exists(lag))(lambda: dq_copy(lag, j).start())

    tri = lax.broadcasted_iota(jnp.int32, (chunk, chunk), 0) <= lax.broadcasted_iota(
        jnp.int32, (chunk, chunk), 1
    )
    dk[...] = jnp.zeros_like(dk)
    dv[...] = jnp.zeros_like(dv)
    for j in range(CHUNKS):
        terms(0, j, 0, (j + 1) * chunk)

    def step_of(n, _):
        qg_arrived(2, n)
        pl.when(qg_goes[2])(lambda: qg_copy(2, n).start())
        pl.when(qg_goes[3])(lambda: qg_copy(3, n).start())
        terms(2, n, 0, rows)
        qg_arrived(1, n)
        terms(1, n, 0, rows)

        @pl.when(even)
        def _():
            qg_arrived(3, n)
            terms(3, n, 0, rows)

        return 0

    lax.fori_loop(0, CHUNKS, step_of, 0)

    for step in range(1, head_n):
        w_copy(step, other(step)).wait_recv()
        w_share(step, other(step), core).start()

    wide = {0: (0, 1), 1: (1, 2)}

    def g_copy(which, r, place, to):
        first_col, cols = wide[which]
        span = pl.ds(first_col * width, cols * width)
        return send(
            gs.at[r, :, span], gr.at[place, :, span],
            g_send.at[which, r], g_recv.at[which, place], me, to,
        )

    def hand_over(which, r, value):
        first_col, cols = wide[which]
        span = slice(first_col * width, (first_col + cols) * width)

        @pl.when(head == r)
        def _():
            gr[head, :, span] = value

        @pl.when(head != r)
        def _():
            gs[r, :, span] = value
            g_copy(which, r, head, r).start()

    def finish_queries(r):
        own = slice(r * chunk, (r + 1) * chunk)
        total = dq[own, :]
        for lag in range(1, 4):
            pl.when(exists(-lag))(lambda: dq_copy(lag, r).wait_recv())
            total += dq_in[lag - 1, own, :].astype(F32)
        hand_over(0, r, total.astype(BF16))

    def finish_keys(r):
        own = slice(r * chunk, (r + 1) * chunk)
        hand_over(
            1, r,
            beside((dk[own, :] * (scale * norm)).astype(BF16), (dv[own, :] * norm).astype(BF16)),
        )

    @pl.when(even)
    def _():
        for r in range(CHUNKS):
            finish_keys(r)
        for r in range(CHUNKS):
            finish_queries(r)

    @pl.when(odd)
    def _():
        for r in range(CHUNKS):
            qg_arrived(3, r)
            terms(3, r, r * chunk, rows)
            finish_keys(r)
            finish_queries(r)

    for step in range(1, head_n):
        w_share(step, other(step), 1 - core).wait_recv()
    total = dot(gr[head], wg[head], NT)
    for step in range(1, head_n):
        place = other(step)
        for which in (0, 1):
            g_copy(which, 0, place, place).wait_recv()
        total += dot(gr[place], wg[place], NT)
    out_ref[...] = total

    for step in range(1, head_n):
        w_copy(step, head).wait_send()
        w_share(step, other(step), core).wait_send()
        for which in (0, 1):
            g_copy(which, other(step), head, other(step)).wait_send()
    for kind in range(4):

        @pl.when(qg_goes[kind])
        def _():
            for j in range(CHUNKS):
                qg_copy(kind, j).wait_send()

    for lag in range(1, 4):

        @pl.when(exists(lag))
        def _():
            for j in range(CHUNKS):
                dq_copy(lag, j).wait_send()


def shards(seq_n, head_n, queries, keys, values, out_grad, lengths, w_proj):
    rows, width = queries.shape
    model = w_proj.shape[1]
    hbm = pl.BlockSpec(memory_space=pl.ANY)
    dma = pltpu.SemaphoreType.DMA
    return pl.pallas_call(
        functools.partial(kernel, seq_n, head_n),
        out_shape=jax.ShapeDtypeStruct((rows // head_n, model), F32),
        in_specs=[hbm] * 4 + [pl.BlockSpec(memory_space=pltpu.SMEM), hbm],
        out_specs=pl.BlockSpec(memory_space=pltpu.VMEM),
        scratch_shapes=[
            pltpu.VMEM((2, rows, width), BF16),
            pltpu.VMEM((4, 2, rows, width), BF16),
            pltpu.VMEM((rows, width), BF16),
            pltpu.VMEM((4, rows, width), BF16),
            pltpu.VMEM((rows, width), F32),
            pltpu.VMEM((rows, width), F32),
            pltpu.VMEM((rows, width), F32),
            pltpu.VMEM((3, rows, width), BF16),
            pltpu.VMEM((3, rows, width), BF16),
            pltpu.VMEM((head_n, rows // head_n, 3 * width), BF16),
            pltpu.VMEM((head_n, rows // head_n, 3 * width), BF16),
            pltpu.VMEM((head_n, model, 3 * width), BF16),
            dma((7,)),
            dma((4, CHUNKS)),
            dma((4, CHUNKS)),
            dma((3, CHUNKS)),
            dma((3, CHUNKS)),
            dma((2, head_n - 1)),
            dma((2, head_n)),
            dma((2, head_n)),
            dma((2, head_n)),
        ],
        compiler_params=pltpu.CompilerParams(
            collective_id=0, has_side_effects=True, vmem_limit_bytes=60 << 20
        ),
    )(queries, keys, values, out_grad, lengths, w_proj)


def solution(mesh):
    return jax.shard_map(
        functools.partial(shards, mesh.shape["seq"], mesh.shape["head"]),
        mesh=mesh,
        in_specs=(
            P("seq", "head"),
            P("seq", "head"),
            P("seq", "head"),
            P("seq", "head"),
            P(),
            P(None, None, "head"),
        ),
        out_specs=P(("seq", "head"), None),
        check_vma=False,
    )
```

```python
import functools
import math

import jax
import jax.numpy as jnp
from jax import lax
from jax.experimental import pallas as pl
from jax.experimental.pallas import tpu as pltpu
from jax.sharding import PartitionSpec as P

MAXLEN = 3072
CHUNKS = 4
FAR = 8192.0
F32 = jnp.float32
BF16 = jnp.bfloat16
NT = (((1,), (1,)), ((), ()))
NN = (((1,), (0,)), ((), ()))
TN = (((0,), (0,)), ((), ()))


def dot(a, b, dims):
    return lax.dot_general(a, b, dims, preferred_element_type=F32)


def beside(a, b):
    return jnp.concatenate([a, b], axis=1)


def kernel(
    seq_n, head_n,
    q_in, k_in, v_in, g_in, len_hbm, w_in,
    out_ref,
    kv, qg, ka, qa, dq, dk, dv, dq_out, dq_in, gs, gr, wg,
    load_sem, qg_send, qg_recv, dq_send, dq_recv, w_send, w_recv, g_send, g_recv, len_in,
):
    rows, width = q_in.shape
    chunk = rows // CHUNKS
    scale = width ** -0.5
    norm = 1.0 / math.sqrt(MAXLEN)
    me = lax.axis_index("seq")
    head = lax.axis_index("head")
    even = lax.rem(me, 2) == 0
    odd = lax.rem(me, 2) == 1

    def exists(step):
        return (me + step >= 0) & (me + step < seq_n)

    def other(step):
        return lax.rem(head + step, head_n)

    loads = [
        pltpu.make_async_copy(k_in, kv.at[0], load_sem.at[0]),
        pltpu.make_async_copy(v_in, kv.at[1], load_sem.at[1]),
        pltpu.make_async_copy(q_in, qg.at[0, 0], load_sem.at[2]),
        pltpu.make_async_copy(g_in, qg.at[0, 1], load_sem.at[3]),
    ] + [
        pltpu.make_async_copy(
            w_in.at[c], wg.at[head, :, pl.ds(c * width, width)], load_sem.at[4 + c]
        )
        for c in range(3)
    ] + [pltpu.make_async_copy(len_hbm, len_in, load_sem.at[7])]
    for load in loads:
        load.start()

    barrier = pltpu.get_barrier_semaphore()
    for step in (-3, -2, -1, 1, 2, 3):

        @pl.when(exists(step))
        def _():
            pl.semaphore_signal(
                barrier, inc=1, device_id=(me + step, head), device_id_type=pl.DeviceIdType.MESH
            )

    for step in range(1, head_n):
        pl.semaphore_signal(
            barrier, inc=1, device_id=(me, other(step)), device_id_type=pl.DeviceIdType.MESH
        )
    missing = jnp.maximum(3 - me, 0) + jnp.maximum(me + 4 - seq_n, 0)
    pl.semaphore_wait(barrier, 6 + head_n - 1 - missing)

    core = lax.rem(me, 2)
    sibling = me + 1 - 2 * core

    def send(src, dst, send_sem, recv_sem, seq_to, head_to):
        return pltpu.make_async_remote_copy(
            src_ref=src, dst_ref=dst, send_sem=send_sem, recv_sem=recv_sem,
            device_id=(seq_to, head_to), device_id_type=pl.DeviceIdType.MESH,
        )

    def part(buf, lag, j):
        return buf.at[lag, :, pl.ds(j * chunk, chunk), :]

    def qg_copy(kind, j):
        src, dst, step = ((0, 2, -2), (0, 1, -1), (2, 3, -1), (2, 1, 1))[kind]
        return send(part(qg, src, j), part(qg, dst, j), qg_send.at[kind, j], qg_recv.at[dst, j], me + step, head)

    def qg_arrived(lag, j):
        pl.when(exists(lag))(lambda: qg_copy({1: 1, 2: 0, 3: 2}[lag], j).wait_recv())

    def dq_copy(lag, j):
        here = pl.ds(j * chunk, chunk)
        return send(
            dq_out.at[lag - 1, here, :], dq_in.at[lag - 1, here, :],
            dq_send.at[lag - 1, j], dq_recv.at[lag - 1, j], sibling if lag == 2 else me + lag, head,
        )

    qg_goes = (exists(-2), odd, exists(2) & exists(-1), even & exists(2))
    for load in loads[2:4]:
        load.wait()
    for n in range(CHUNKS):
        pl.when(qg_goes[0])(lambda: qg_copy(0, n).start())
        pl.when(qg_goes[1])(lambda: qg_copy(1, n).start())
    for load in loads[:2] + loads[4:]:
        load.wait()

    half = w_in.shape[1] // 2

    def w_part(place, which):
        return wg.at[place, pl.ds(which * half, half), :]

    def w_copy(step, place):
        ref = w_part(place, core)
        return send(ref, ref, w_send.at[0, step - 1], w_recv.at[0, place], me, other(step))

    def w_share(step, place, which):
        ref = w_part(place, which)
        return send(ref, ref, w_send.at[1, step - 1], w_recv.at[1, place], sibling, head)

    for step in range(1, head_n):
        w_copy(step, head).start()

    lane = lax.broadcasted_iota(jnp.int32, (1, width), 1)

    def user_step(u, carry):
        end, starts, ends = carry
        later = end + len_in[u]
        return (later, jnp.where(lane == u, end, starts), jnp.where(lane == u, later, ends))

    zero = jnp.zeros((1, width), jnp.int32)
    _, starts, ends = lax.fori_loop(0, len_in.shape[0], user_step, (jnp.int32(0), zero, zero))
    offsets = lax.broadcasted_iota(jnp.int32, (rows, width), 0)

    def belongs(step):
        pos = offsets + (me + step) * rows
        return (pos >= starts) & (pos < ends)

    ka[...] = jnp.where(belongs(0), 0.0, -FAR).astype(BF16)
    for lag in range(4):
        qa[lag] = jnp.where(belongs(lag), 1.0, 0.0).astype(BF16)

    for lag in range(1, 4):

        @pl.when(jnp.logical_not(exists(-lag)))
        def _():
            if lag != 2:
                dq_in[lag - 1] = jnp.zeros(dq_in.shape[1:], BF16)

        @pl.when(jnp.logical_not(exists(lag)))
        def _():
            qg[lag] = jnp.zeros(qg.shape[1:], BF16)

    def gates(scores, d_weights):
        s = scores * scale
        p = jax.nn.sigmoid(s)
        a = s * p
        ds = (p + a * (1.0 - p)) * d_weights
        return a.astype(BF16), ds.astype(BF16)

    def terms(lag, j, r0, r1):
        here = pl.ds(j * chunk, chunk)
        own = slice(r0, r1)
        queries = qg[lag, 0, here, :]
        grads = qg[lag, 1, here, :]
        keys = kv[0, own, :]
        s = dot(beside(keys, ka[own, :]), beside(queries, qa[lag, here, :]), NT)
        if lag == 0:
            last = jnp.where(tri, s[r1 - chunk :, :], -FAR)
            s = last if r1 == chunk else jnp.concatenate([s[: r1 - chunk, :], last], axis=0)
        d = dot(kv[1, own, :], grads, NT)
        a, ds = gates(s, d)
        dk[own, :] += dot(ds, queries, NN)
        dv[own, :] += dot(a, grads, NN)
        partial = dot(ds, keys, TN) * (scale * norm)
        if lag == 0:
            dq[here, :] = partial
            return
        dq_out[lag - 1, here, :] = partial.astype(BF16)
        if lag == 2:
            dq_copy(2, j).start()

    def dq_goes(lag, j):
        pl.when(exists(lag))(lambda: dq_copy(lag, j).start())

    def dq_joined(lag, j):
        here = pl.ds(j * chunk, chunk)
        dq_copy(2, j).wait_recv()
        total = dq_out[lag - 1, here, :].astype(F32) + dq_in[1, here, :].astype(F32)
        dq_out[lag - 1, here, :] = total.astype(BF16)
        dq_goes(lag, j)

    tri = lax.broadcasted_iota(jnp.int32, (chunk, chunk), 0) <= lax.broadcasted_iota(
        jnp.int32, (chunk, chunk), 1
    )
    dk[...] = jnp.zeros_like(dk)
    dv[...] = jnp.zeros_like(dv)
    for j in range(CHUNKS):
        terms(0, j, 0, (j + 1) * chunk)

    def step_of(n, _):
        qg_arrived(2, n)
        pl.when(qg_goes[2])(lambda: qg_copy(2, n).start())
        pl.when(qg_goes[3])(lambda: qg_copy(3, n).start())
        terms(2, n, 0, rows)
        qg_arrived(1, n)
        terms(1, n, 0, rows)

        @pl.when(even)
        def _():
            dq_goes(1, n)
            qg_arrived(3, n)
            terms(3, n, 0, rows)
            dq_joined(3, n)

        @pl.when(odd)
        def _():
            dq_joined(1, n)

        return 0

    lax.fori_loop(0, CHUNKS, step_of, 0)

    for step in range(1, head_n):
        w_copy(step, other(step)).wait_recv()
        w_share(step, other(step), core).start()

    wide = {0: (0, 1), 1: (1, 2)}

    def g_copy(which, r, place, to):
        first_col, cols = wide[which]
        span = pl.ds(first_col * width, cols * width)
        return send(
            gs.at[r, :, span], gr.at[place, :, span],
            g_send.at[which, r], g_recv.at[which, place], me, to,
        )

    def hand_over(which, r, value):
        first_col, cols = wide[which]
        span = slice(first_col * width, (first_col + cols) * width)

        @pl.when(head == r)
        def _():
            gr[head, :, span] = value

        @pl.when(head != r)
        def _():
            gs[r, :, span] = value
            g_copy(which, r, head, r).start()

    def finish_queries(r):
        own = slice(r * chunk, (r + 1) * chunk)
        total = dq[own, :]
        for lag in (1, 3):
            pl.when(exists(-lag))(lambda: dq_copy(lag, r).wait_recv())
            total += dq_in[lag - 1, own, :].astype(F32)
        hand_over(0, r, total.astype(BF16))

    def finish_keys(r):
        own = slice(r * chunk, (r + 1) * chunk)
        hand_over(
            1, r,
            beside((dk[own, :] * (scale * norm)).astype(BF16), (dv[own, :] * norm).astype(BF16)),
        )

    @pl.when(even)
    def _():
        for r in range(CHUNKS):
            finish_keys(r)
        for r in range(CHUNKS):
            finish_queries(r)

    @pl.when(odd)
    def _():
        for r in range(CHUNKS):
            qg_arrived(3, r)
            terms(3, r, r * chunk, rows)
            dq_goes(3, r)
            finish_keys(r)
            finish_queries(r)

    for step in range(1, head_n):
        w_share(step, other(step), 1 - core).wait_recv()
    total = dot(gr[head], wg[head], NT)
    for step in range(1, head_n):
        place = other(step)
        for which in (0, 1):
            g_copy(which, 0, place, place).wait_recv()
        total += dot(gr[place], wg[place], NT)
    out_ref[...] = total

    for step in range(1, head_n):
        w_copy(step, head).wait_send()
        w_share(step, other(step), core).wait_send()
        for which in (0, 1):
            g_copy(which, other(step), head, other(step)).wait_send()
    for kind in range(4):

        @pl.when(qg_goes[kind])
        def _():
            for j in range(CHUNKS):
                qg_copy(kind, j).wait_send()

    for j in range(CHUNKS):
        dq_copy(2, j).wait_send()
    for lag in (1, 3):

        @pl.when(exists(lag))
        def _():
            for j in range(CHUNKS):
                dq_copy(lag, j).wait_send()


def shards(seq_n, head_n, queries, keys, values, out_grad, lengths, w_proj):
    rows, width = queries.shape
    model = w_proj.shape[1]
    hbm = pl.BlockSpec(memory_space=pl.ANY)
    dma = pltpu.SemaphoreType.DMA
    operands = [
        pltpu.with_memory_space_constraint(x, pltpu.HBM)
        for x in (queries, keys, values, out_grad, lengths, w_proj)
    ]
    return pl.pallas_call(
        functools.partial(kernel, seq_n, head_n),
        out_shape=jax.ShapeDtypeStruct((rows // head_n, model), F32),
        in_specs=[hbm] * 6,
        out_specs=pl.BlockSpec(memory_space=pltpu.VMEM),
        scratch_shapes=[
            pltpu.VMEM((2, rows, width), BF16),
            pltpu.VMEM((4, 2, rows, width), BF16),
            pltpu.VMEM((rows, width), BF16),
            pltpu.VMEM((4, rows, width), BF16),
            pltpu.VMEM((rows, width), F32),
            pltpu.VMEM((rows, width), F32),
            pltpu.VMEM((rows, width), F32),
            pltpu.VMEM((3, rows, width), BF16),
            pltpu.VMEM((3, rows, width), BF16),
            pltpu.VMEM((head_n, rows // head_n, 3 * width), BF16),
            pltpu.VMEM((head_n, rows // head_n, 3 * width), BF16),
            pltpu.VMEM((head_n, model, 3 * width), BF16),
            dma((8,)),
            dma((4, CHUNKS)),
            dma((4, CHUNKS)),
            dma((3, CHUNKS)),
            dma((3, CHUNKS)),
            dma((2, head_n - 1)),
            dma((2, head_n)),
            dma((2, head_n)),
            dma((2, head_n)),
            pltpu.SMEM(lengths.shape, jnp.int32),
        ],
        compiler_params=pltpu.CompilerParams(
            collective_id=0, has_side_effects=True, vmem_limit_bytes=48 << 20
        ),
    )(*operands)


def solution(mesh):
    return jax.shard_map(
        functools.partial(shards, mesh.shape["seq"], mesh.shape["head"]),
        mesh=mesh,
        in_specs=(
            P("seq", "head"),
            P("seq", "head"),
            P("seq", "head"),
            P("seq", "head"),
            P(),
            P(None, None, "head"),
        ),
        out_specs=P(("seq", "head"), None),
        check_vma=False,
    )
```

```python
import functools
import math

import jax
import jax.numpy as jnp
from jax import lax
from jax.experimental import pallas as pl
from jax.experimental.pallas import tpu as pltpu
from jax.sharding import PartitionSpec as P

MAXLEN = 3072
CHUNKS = 4
FAR = 8192.0
F32 = jnp.float32
BF16 = jnp.bfloat16
NT = (((1,), (1,)), ((), ()))
NN = (((1,), (0,)), ((), ()))
TN = (((0,), (0,)), ((), ()))


def dot(a, b, dims):
    return lax.dot_general(a, b, dims, preferred_element_type=F32)


def beside(a, b):
    return jnp.concatenate([a, b], axis=1)


def kernel(
    seq_n, head_n,
    q_in, k_in, v_in, g_in, len_hbm, w_in,
    out_ref,
    kv, qg, ka, qa, dq, dk, dv, dq_out, dq_in, gs, gr, wg,
    load_sem, qg_send, qg_recv, dq_send, dq_recv, w_send, w_recv, g_send, g_recv, len_in,
):
    rows, width = q_in.shape
    chunk = rows // CHUNKS
    scale = width ** -0.5
    norm = 1.0 / math.sqrt(MAXLEN)
    me = lax.axis_index("seq")
    head = lax.axis_index("head")
    even = lax.rem(me, 2) == 0
    odd = lax.rem(me, 2) == 1

    def exists(step):
        return (me + step >= 0) & (me + step < seq_n)

    def other(step):
        return lax.rem(head + step, head_n)

    loads = [
        pltpu.make_async_copy(k_in, kv.at[0], load_sem.at[0]),
        pltpu.make_async_copy(v_in, kv.at[1], load_sem.at[1]),
        pltpu.make_async_copy(q_in, qg.at[0, 0], load_sem.at[2]),
        pltpu.make_async_copy(g_in, qg.at[0, 1], load_sem.at[3]),
    ] + [
        pltpu.make_async_copy(
            w_in.at[c], wg.at[head, :, pl.ds(c * width, width)], load_sem.at[4 + c]
        )
        for c in range(3)
    ] + [pltpu.make_async_copy(len_hbm, len_in, load_sem.at[7])]
    for load in loads:
        load.start()

    barrier = pltpu.get_barrier_semaphore()
    for step in (-3, -2, -1, 1, 2, 3):

        @pl.when(exists(step))
        def _():
            pl.semaphore_signal(
                barrier, inc=1, device_id=(me + step, head), device_id_type=pl.DeviceIdType.MESH
            )

    for step in range(1, head_n):
        pl.semaphore_signal(
            barrier, inc=1, device_id=(me, other(step)), device_id_type=pl.DeviceIdType.MESH
        )
    missing = jnp.maximum(3 - me, 0) + jnp.maximum(me + 4 - seq_n, 0)
    pl.semaphore_wait(barrier, 6 + head_n - 1 - missing)

    core = lax.rem(me, 2)
    sibling = me + 1 - 2 * core

    def send(src, dst, send_sem, recv_sem, seq_to, head_to):
        return pltpu.make_async_remote_copy(
            src_ref=src, dst_ref=dst, send_sem=send_sem, recv_sem=recv_sem,
            device_id=(seq_to, head_to), device_id_type=pl.DeviceIdType.MESH,
        )

    def part(buf, lag, j):
        return buf.at[lag, :, pl.ds(j * chunk, chunk), :]

    def qg_copy(kind, j):
        src, dst, step = ((0, 2, -2), (0, 1, -1), (2, 3, -1), (2, 1, 1))[kind]
        return send(part(qg, src, j), part(qg, dst, j), qg_send.at[kind, j], qg_recv.at[dst, j], me + step, head)

    def qg_arrived(lag, j):
        pl.when(exists(lag))(lambda: qg_copy({1: 1, 2: 0, 3: 2}[lag], j).wait_recv())

    def dq_copy(lag, j):
        here = pl.ds(j * chunk, chunk)
        return send(
            dq_out.at[lag - 1, here, :], dq_in.at[lag - 1, here, :],
            dq_send.at[lag - 1, j], dq_recv.at[lag - 1, j], sibling if lag == 2 else me + lag, head,
        )

    qg_goes = (exists(-2), odd, exists(2) & exists(-1), even & exists(2))
    for load in loads[2:4]:
        load.wait()
    for n in range(CHUNKS):
        pl.when(qg_goes[0])(lambda: qg_copy(0, n).start())
        pl.when(qg_goes[1])(lambda: qg_copy(1, n).start())
    for load in loads[:2] + loads[4:]:
        load.wait()

    half = w_in.shape[1] // 2

    def w_part(place, which):
        return wg.at[place, pl.ds(which * half, half), :]

    def w_copy(step, place):
        ref = w_part(place, core)
        return send(ref, ref, w_send.at[0, step - 1], w_recv.at[0, place], me, other(step))

    def w_share(step, place, which):
        ref = w_part(place, which)
        return send(ref, ref, w_send.at[1, step - 1], w_recv.at[1, place], sibling, head)

    for step in range(1, head_n):
        w_copy(step, head).start()

    lane = lax.broadcasted_iota(jnp.int32, (1, width), 1)

    def user_step(u, carry):
        end, starts, ends = carry
        later = end + len_in[u]
        return (later, jnp.where(lane == u, end, starts), jnp.where(lane == u, later, ends))

    zero = jnp.zeros((1, width), jnp.int32)
    _, starts, ends = lax.fori_loop(0, len_in.shape[0], user_step, (jnp.int32(0), zero, zero))
    offsets = lax.broadcasted_iota(jnp.int32, (rows, width), 0)

    def belongs(step):
        pos = offsets + (me + step) * rows
        return (pos >= starts) & (pos < ends)

    ka[...] = jnp.where(belongs(0), 0.0, -FAR).astype(BF16)
    for lag in range(4):
        qa[lag] = jnp.where(belongs(lag), 1.0, 0.0).astype(BF16)

    for lag in range(1, 4):

        @pl.when(jnp.logical_not(exists(-lag)))
        def _():
            if lag != 2:
                dq_in[lag - 1] = jnp.zeros(dq_in.shape[1:], BF16)

        @pl.when(jnp.logical_not(exists(lag)))
        def _():
            qg[lag] = jnp.zeros(qg.shape[1:], BF16)

    def gates(scores, d_weights):
        s = scores * scale
        p = jax.nn.sigmoid(s)
        a = s * p
        ds = (p + a * (1.0 - p)) * d_weights
        return a.astype(BF16), ds.astype(BF16)

    def terms(lag, j, r0, r1):
        here = pl.ds(j * chunk, chunk)
        own = slice(r0, r1)
        queries = qg[lag, 0, here, :]
        grads = qg[lag, 1, here, :]
        keys = kv[0, own, :]
        s = dot(beside(keys, ka[own, :]), beside(queries, qa[lag, here, :]), NT)
        if lag == 0:
            last = jnp.where(tri, s[r1 - chunk :, :], -FAR)
            s = last if r1 == chunk else jnp.concatenate([s[: r1 - chunk, :], last], axis=0)
        d = dot(kv[1, own, :], grads, NT)
        a, ds = gates(s, d)
        dk[own, :] += dot(ds, queries, NN)
        dv[own, :] += dot(a, grads, NN)
        partial = dot(ds, keys, TN) * (scale * norm)
        if lag == 0:
            dq[here, :] = partial
            return
        dq_out[lag - 1, here, :] = partial.astype(BF16)
        if lag == 2:
            dq_copy(2, j).start()

    def dq_goes(lag, j):
        pl.when(exists(lag))(lambda: dq_copy(lag, j).start())

    def dq_joined(lag, j):
        here = pl.ds(j * chunk, chunk)
        dq_copy(2, j).wait_recv()
        total = dq_out[lag - 1, here, :].astype(F32) + dq_in[1, here, :].astype(F32)
        dq_out[lag - 1, here, :] = total.astype(BF16)
        dq_goes(lag, j)

    tri = lax.broadcasted_iota(jnp.int32, (chunk, chunk), 0) <= lax.broadcasted_iota(
        jnp.int32, (chunk, chunk), 1
    )
    dk[...] = jnp.zeros_like(dk)
    dv[...] = jnp.zeros_like(dv)
    for j in range(CHUNKS):
        terms(0, j, 0, (j + 1) * chunk)

    def step_of(n, _):
        qg_arrived(2, n)
        pl.when(qg_goes[2])(lambda: qg_copy(2, n).start())
        pl.when(qg_goes[3])(lambda: qg_copy(3, n).start())
        terms(2, n, 0, rows)
        qg_arrived(1, n)
        terms(1, n, 0, rows)

        @pl.when(even)
        def _():
            dq_goes(1, n)
            qg_arrived(3, n)
            terms(3, n, 0, rows)
            dq_joined(3, n)

        @pl.when(odd)
        def _():
            dq_joined(1, n)

        return 0

    lax.fori_loop(0, CHUNKS, step_of, 0)

    for step in range(1, head_n):
        w_copy(step, other(step)).wait_recv()
        w_share(step, other(step), core).start()

    wide = {0: (0, 1), 1: (1, 2)}

    def g_copy(which, r, place, to):
        first_col, cols = wide[which]
        span = pl.ds(first_col * width, cols * width)
        return send(
            gs.at[r, :, span], gr.at[place, :, span],
            g_send.at[which, r], g_recv.at[which, place], me, to,
        )

    def hand_over(which, r, value):
        first_col, cols = wide[which]
        span = slice(first_col * width, (first_col + cols) * width)

        @pl.when(head == r)
        def _():
            gr[head, :, span] = value

        @pl.when(head != r)
        def _():
            gs[r, :, span] = value
            g_copy(which, r, head, r).start()

    def finish_queries(r):
        own = slice(r * chunk, (r + 1) * chunk)
        total = dq[own, :]
        for lag in (1, 3):
            pl.when(exists(-lag))(lambda: dq_copy(lag, r).wait_recv())
            total += dq_in[lag - 1, own, :].astype(F32)
        hand_over(0, r, total.astype(BF16))

    def finish_keys(r):
        own = slice(r * chunk, (r + 1) * chunk)
        hand_over(
            1, r,
            beside((dk[own, :] * (scale * norm)).astype(BF16), (dv[own, :] * norm).astype(BF16)),
        )

    @pl.when(even)
    def _():
        for r in range(CHUNKS):
            finish_keys(r)
        for r in range(CHUNKS):
            finish_queries(r)

    @pl.when(odd)
    def _():
        for r in range(CHUNKS):
            qg_arrived(3, r)
            terms(3, r, r * chunk, rows)
            dq_goes(3, r)
            finish_keys(r)
        for r in range(CHUNKS):
            finish_queries(r)

    for step in range(1, head_n):
        w_share(step, other(step), 1 - core).wait_recv()
    total = dot(gr[head], wg[head], NT)
    for step in range(1, head_n):
        place = other(step)
        for which in (0, 1):
            g_copy(which, 0, place, place).wait_recv()
        total += dot(gr[place], wg[place], NT)
    out_ref[...] = total

    for step in range(1, head_n):
        w_copy(step, head).wait_send()
        w_share(step, other(step), core).wait_send()
        for which in (0, 1):
            g_copy(which, other(step), head, other(step)).wait_send()
    for kind in range(4):

        @pl.when(qg_goes[kind])
        def _():
            for j in range(CHUNKS):
                qg_copy(kind, j).wait_send()

    for j in range(CHUNKS):
        dq_copy(2, j).wait_send()
    for lag in (1, 3):

        @pl.when(exists(lag))
        def _():
            for j in range(CHUNKS):
                dq_copy(lag, j).wait_send()


def shards(seq_n, head_n, queries, keys, values, out_grad, lengths, w_proj):
    rows, width = queries.shape
    model = w_proj.shape[1]
    hbm = pl.BlockSpec(memory_space=pl.ANY)
    dma = pltpu.SemaphoreType.DMA
    operands = [
        pltpu.with_memory_space_constraint(x, pltpu.HBM)
        for x in (queries, keys, values, out_grad, lengths, w_proj)
    ]
    return pl.pallas_call(
        functools.partial(kernel, seq_n, head_n),
        out_shape=jax.ShapeDtypeStruct((rows // head_n, model), F32),
        in_specs=[hbm] * 6,
        out_specs=pl.BlockSpec(memory_space=pltpu.VMEM),
        scratch_shapes=[
            pltpu.VMEM((2, rows, width), BF16),
            pltpu.VMEM((4, 2, rows, width), BF16),
            pltpu.VMEM((rows, width), BF16),
            pltpu.VMEM((4, rows, width), BF16),
            pltpu.VMEM((rows, width), F32),
            pltpu.VMEM((rows, width), F32),
            pltpu.VMEM((rows, width), F32),
            pltpu.VMEM((3, rows, width), BF16),
            pltpu.VMEM((3, rows, width), BF16),
            pltpu.VMEM((head_n, rows // head_n, 3 * width), BF16),
            pltpu.VMEM((head_n, rows // head_n, 3 * width), BF16),
            pltpu.VMEM((head_n, model, 3 * width), BF16),
            dma((8,)),
            dma((4, CHUNKS)),
            dma((4, CHUNKS)),
            dma((3, CHUNKS)),
            dma((3, CHUNKS)),
            dma((2, head_n - 1)),
            dma((2, head_n)),
            dma((2, head_n)),
            dma((2, head_n)),
            pltpu.SMEM(lengths.shape, jnp.int32),
        ],
        compiler_params=pltpu.CompilerParams(
            collective_id=0, has_side_effects=True, vmem_limit_bytes=48 << 20
        ),
    )(*operands)


def solution(mesh):
    return jax.shard_map(
        functools.partial(shards, mesh.shape["seq"], mesh.shape["head"]),
        mesh=mesh,
        in_specs=(
            P("seq", "head"),
            P("seq", "head"),
            P("seq", "head"),
            P("seq", "head"),
            P(),
            P(None, None, "head"),
        ),
        out_specs=P(("seq", "head"), None),
        check_vma=False,
    )
```
